32 devices in a mesh: row: 8 (over y, x, core), col: 4 (over z).
Axes of the slice: x: 2, y: 2, z: 4, core: 2. Of those that a mesh axis runs over, the one named last changes fastest.
Arguments:
- kernel: float32 [16384, 16384], P('row', 'col'), may hold values from -7 to 7, as said below
- nugget: float32 [16384], P('row'), may hold values from 0.25 to 1
Outputs:
- factored: float32 [16384, 16384], P('row', 'col')
The draws below stay inside these ranges and needn't reach their ends.
Inputs may be any that keep to these rules, and one draw needn't show every extreme that they name: In matrix order the kernel is symmetric and positive semidefinite.
All inputs are finite; a program needn't handle non-finite values.
Results may differ from the reference program's by a relative error of at most 0.0018.
Values may be sent and summed in bfloat16 or wider, within the bound.
No kernel may reach another device: no remote copies, remote signals or barrier semaphores. Data moves between devices by JAX's collectives and lax.ppermute only.
A program may use at most 192 MiB of HBM per device.

```python
import math
import jax
import jax.numpy as jnp
from jax import lax

N = 16384
B = 256
STEPS = 7
DIM = 64
FEAT = 4096
ROWS_DEV = 2048
COLS_DEV = 4096


def natural_of_stored_drawn(total_count, per_device, tile_width):
    stored = jnp.arange(total_count, dtype=jnp.int32)
    grid_size = total_count // per_device
    device = stored // per_device
    within = stored % per_device
    return (within // tile_width * grid_size + device) * tile_width + within % tile_width


def draw_kernel(key, part):
    gen_key, dim_key, freq_key = jax.random.split(key, 3)
    generator = jax.random.randint(gen_key, (DIM,), 1, N)
    dim_pick = jax.random.randint(dim_key, (2, FEAT), 0, DIM)
    frequency = jax.random.randint(freq_key, (2, FEAT), 1, 17).astype(jnp.float32)

    def features(natural):
        points = (natural[:, None] * generator[None, :] % N).astype(jnp.float32) / N
        folded = 1.0 - jnp.abs(2.0 * points - 1.0)
        cos_first = jnp.cos(math.pi * frequency[0][None, :] * jnp.take(folded, dim_pick[0], axis=1))
        cos_second = jnp.cos(math.pi * frequency[1][None, :] * jnp.take(folded, dim_pick[1], axis=1))
        return cos_first * cos_second
    row_features = features(natural_of_stored_drawn(N, ROWS_DEV, B))
    col_features = features(natural_of_stored_drawn(N, COLS_DEV, B))
    return jnp.dot(row_features, col_features.T, precision=lax.Precision.HIGHEST) * (4.0 / FEAT)


def steps_of(key, shape, cuts, low, largest):
    loudness, own = 1.0, jax.random.fold_in(key, 6)
    for axis_at, parts in cuts:
        heights = jnp.exp(jax.random.uniform(jax.random.fold_in(own, axis_at), (parts,), jnp.float32, low / len(cuts), largest / len(cuts)))
        loudness = loudness * jnp.repeat(heights, shape[axis_at] // parts).reshape([-1 if axis == axis_at else 1 for axis in range(len(shape))])
    return loudness


def setup_inputs(seed: int = 0) -> dict:
    streams_of = jax.random.split(jax.random.key(seed), 3)
    kernel = draw_kernel(jax.random.fold_in(streams_of[2], 71), 0)
    nugget = jnp.clip(jnp.exp(math.log(1.0) - 1.3862944 * jax.random.uniform(streams_of[1], (N,), jnp.float32) ** steps_of(streams_of[1], (N,), ((0, 8),), -0.2, 0.2)), 0.25, 1.0)
    return {"kernel": kernel, "nugget": nugget}


def stored_of_natural(total_count, per_device, tile_width):
    natural = jnp.arange(total_count, dtype=jnp.int32)
    grid_size = total_count // per_device
    tile_index = natural // tile_width
    return tile_index % grid_size * per_device + tile_index // grid_size * tile_width + natural % tile_width

def natural_of_stored(total_count, per_device, tile_width):
    stored = jnp.arange(total_count, dtype=jnp.int32)
    grid_size = total_count // per_device
    device = stored // per_device
    within = stored % per_device
    return (within // tile_width * grid_size + device) * tile_width + within % tile_width

def reference(kernel, nugget):
    from_rows = stored_of_natural(N, ROWS_DEV, B)
    from_cols = stored_of_natural(N, COLS_DEV, B)
    matrix = jnp.take(jnp.take(kernel, from_rows, axis=0), from_cols, axis=1)
    diagonal_at = jnp.arange(N, dtype=jnp.int32)
    matrix = matrix.at[diagonal_at, diagonal_at].add(jnp.take(nugget, from_rows))
    for panel_step in range(STEPS):
        low_edge = panel_step * B
        high_edge = low_edge + B
        factor = jnp.linalg.cholesky(matrix[low_edge:high_edge, low_edge:high_edge])
        solved = lax.linalg.triangular_solve(factor, matrix[high_edge:, low_edge:high_edge], left_side=False, lower=True, transpose_a=True)
        rounded = solved.astype(jnp.bfloat16)
        product = jnp.dot(rounded.astype(jnp.float32), rounded.T.astype(jnp.float32), preferred_element_type=jnp.float32)
        matrix = matrix.at[high_edge:, high_edge:].add(-product)
        matrix = matrix.at[low_edge:high_edge, low_edge:high_edge].set(factor)
        matrix = matrix.at[high_edge:, low_edge:high_edge].set(solved)
        matrix = matrix.at[low_edge:high_edge, high_edge:].set(jnp.float32(0.0))
    to_rows = natural_of_stored(N, ROWS_DEV, B)
    to_cols = natural_of_stored(N, COLS_DEV, B)
    return jnp.take(jnp.take(matrix, to_rows, axis=0), to_cols, axis=1)
```

```python
import functools

import jax
import jax.numpy as jnp
from jax import lax
from jax.experimental import pallas as pl
from jax.experimental.pallas import tpu as pltpu
from jax.sharding import PartitionSpec as P

B = 256
STEPS = 7
FIRST = 4
SUB = 64
VMEM_LIMIT = 56 * 1024 * 1024


def assign_tiles(grid_cols):
    spare = STEPS
    sent, taken = {}, {}
    options = {}
    for a in range(STEPS):
        for b in range(a, STEPS):
            if b == a + grid_cols:
                sent[(a, b)] = (spare, a % grid_cols, 1, False)
                continue
            options[(a, b)] = [(a, b % grid_cols, b // grid_cols, False)]
            if a != b:
                options[(a, b)].append((b, a % grid_cols, a // grid_cols, True))

    def place(pair, seen):
        for option in options[pair]:
            device = option[:2]
            if device in seen:
                continue
            seen.add(device)
            if device not in taken or place(taken[device], seen):
                taken[device] = pair
                sent[pair] = option
                return True
        return False

    for pair in options:
        assert place(pair, set())
    return sent


def split(x):
    hi = x.astype(jnp.bfloat16)
    return hi, (x - hi.astype(jnp.float32)).astype(jnp.bfloat16)


def dot(a, b, dims=(1, 0)):
    return lax.dot_general(a, b, (((dims[0],), (dims[1],)), ((), ())), preferred_element_type=jnp.float32)


def dot_wide(a, b, dims=(1, 0)):
    a_hi, a_lo = split(a)
    b_hi, b_lo = split(b)
    return dot(a_hi, b_hi, dims) + (dot(a_hi, b_lo, dims) + dot(a_lo, b_hi, dims))


def eliminate(block):
    width = block.shape[1]
    count = SUB // 8
    rows = [block[8 * v : 8 * v + 8] for v in range(count)]
    sublane = lax.broadcasted_iota(jnp.int32, (8, width), 0)

    def lane(x, at):
        return jnp.broadcast_to(x[:, at : at + 1], (8, width))

    def row(x, at):
        return jnp.broadcast_to(x[at : at + 1], (8, width))

    for g in range(count):
        cols = [[lane(rows[v], 8 * g + m) for v in range(g, count)] for m in range(8)]
        pivot = {(a, b): row(cols[b][0], a) for b in range(8) for a in range(b, 8)}
        root, low = [None] * 8, {}
        for b in range(8):
            root[b] = lax.rsqrt(pivot[b, b])
            for a in range(b + 1, 8):
                low[a, b] = pivot[a, b] * root[b]
            for a in range(b + 1, 8):
                for c in range(b + 1, a + 1):
                    pivot[a, c] = pivot[a, c] - low[a, b] * low[c, b]
        inv = {}
        for b in range(8):
            inv[b, b] = root[b]
            for a in range(b + 1, 8):
                total = low[a, b] * inv[b, b]
                for m in range(b + 1, a):
                    total = total + low[a, m] * inv[m, b]
                inv[a, b] = -root[a] * total
        solved = None
        for b in range(8):
            coef = jnp.zeros((8, width), jnp.float32)
            for a in range(b, 8):
                coef = jnp.where(sublane == a, inv[a, b], coef)
            term = coef * row(rows[g], b)
            solved = term if solved is None else solved + term
        rows[g] = solved
        if g + 1 < count:
            across = [row(solved, m) for m in range(8)]
            for v in range(g + 1, count):
                total = None
                for m in range(8):
                    factor = inv[m, 0] * cols[0][v - g]
                    for b in range(1, m + 1):
                        factor = factor + inv[m, b] * cols[b][v - g]
                    term = factor * across[m]
                    total = term if total is None else total + term
                rows[v] = rows[v] - total
    return jnp.concatenate(rows, axis=0)


def factor_tile(work):
    eye = (
        lax.broadcasted_iota(jnp.int32, (SUB, 2 * SUB), 0) + SUB
        == lax.broadcasted_iota(jnp.int32, (SUB, 2 * SUB), 1)
    ).astype(jnp.float32)
    left = lax.broadcasted_iota(jnp.int32, (SUB, 2 * SUB), 1) < SUB
    for b in range(B // SUB):
        at = b * SUB
        base = at // (2 * SUB) * (2 * SUB)
        odd = at != base
        pair = work[at : at + SUB, base : base + 2 * SUB]
        if odd:
            pair = pltpu.roll(pair, SUB, 1)
        done = eliminate(jnp.where(left, pair, eye))
        moved = pltpu.roll(done, SUB, 1)
        inverse = moved[:, :SUB]
        end = B + base + 2 * SUB
        solved = dot_wide(inverse, work[at : at + SUB, base:end])
        if at + SUB < B:
            padded = jnp.where(left, 0.0, done) if odd else jnp.where(left, moved, 0.0)
            below = dot_wide(work[at + SUB : B, base : base + 2 * SUB], padded, (1, 1))
            start = (at + SUB) // (2 * SUB) * (2 * SUB)
            work[at + SUB : B, start:end] -= dot_wide(below, solved[:, start - base :])
        work[at : at + SUB, base:end] = solved


def factor_body(tiles_of, count, steps, share, chunk, *refs):
    if tiles_of is None:
        held_ref, refs = refs[0], refs[1:]
    else:
        tiles_ref, wide_ref, refs = refs[0], refs[1], refs[2:]
    rest_ref = None
    if steps < count:
        rest_ref, refs = refs[0], refs[1:]
    col_ref, row_ref, lower_ref, held, panel, work = refs
    edge = count * B
    if tiles_of is None:
        held[...] = held_ref[...]
    else:
        for (a, b), (index, turned) in tiles_of.items():
            tile = tiles_ref[index]
            held[a, :, b * B : (b + 1) * B] = tile.T if turned else tile
        for a in range(count):
            held[a, :, edge:] = wide_ref[a]
    above = lax.broadcasted_iota(jnp.int32, (B, B), 0)
    beside = lax.broadcasted_iota(jnp.int32, (B, B), 1)

    def step(k, carry):
        at = pl.multiple_of(k * B, B)
        work[:, :B] = held[k, :, pl.ds(at, B)]
        work[:, B:] = (above == beside).astype(jnp.float32)
        factor_tile(work)
        lower_ref[k] = jnp.where(above >= beside, work[:, :B].T, 0.0)
        inv_hi, inv_lo = split(work[:, B:])

        def solve(c, carry):
            where = pl.ds(pl.multiple_of(c * chunk, chunk), chunk)
            hi, lo = split(held[k, :, where])
            panel[:, where] = (dot(inv_hi, hi) + (dot(inv_hi, lo) + dot(inv_lo, hi))).astype(jnp.bfloat16)
            return carry

        lax.fori_loop((k + 1) * (B // chunk), (edge + share) // chunk, solve, 0)
        own = panel[:, edge:]
        col_ref[pl.ds(at, B), :] = own
        row_ref[:, pl.ds(at, B)] = own.T

        def reduce(i, carry):
            side = panel[:, pl.ds(pl.multiple_of(i * B, B), B)].T
            held[i] -= dot(side, panel[...])
            return carry

        lax.fori_loop(k + 1, count, reduce, 0)
        return carry

    panel[...] = jnp.zeros_like(panel)
    lax.fori_loop(0, steps, step, 0)
    if rest_ref is not None:
        rest_ref[...] = held[steps:, :, steps * B :]


def factor_group(operands, tiles_of, count, steps, share):
    chunk = min(B, share)
    f32, bf16 = jnp.float32, jnp.bfloat16
    outs = [
        jax.ShapeDtypeStruct((steps * B, share), bf16),
        jax.ShapeDtypeStruct((share, steps * B), bf16),
        jax.ShapeDtypeStruct((steps, B, B), f32),
    ]
    if steps < count:
        left = count - steps
        outs.insert(0, jax.ShapeDtypeStruct((left, B, left * B + share), f32))
    whole = pl.BlockSpec(memory_space=pltpu.VMEM)
    return pl.pallas_call(
        functools.partial(factor_body, tiles_of, count, steps, share, chunk),
        out_shape=outs,
        in_specs=[whole] * len(operands),
        out_specs=[whole] * len(outs),
        scratch_shapes=[
            pltpu.VMEM((count, B, count * B + share), f32),
            pltpu.VMEM((B, count * B + share), bf16),
            pltpu.VMEM((B, 2 * B), f32),
        ],
        compiler_params=pltpu.CompilerParams(vmem_limit_bytes=VMEM_LIMIT),
        cost_estimate=pl.CostEstimate(
            flops=steps * 2 * 10**9, bytes_accessed=16 * 2**20, transcendentals=0
        ),
        name="factor",
    )(*operands)


def trail_body(last, grid_rows, grid_cols, slots, width, *refs):
    place, prev_ref, *sides, col_ref, lower_ref, nugget_ref, out_ref = refs
    row_pos, col_pos = place[0], place[1]
    share = sides[0].shape[0]
    skip = B // width if last else 0
    start = (pl.program_id(0) + skip) * width
    slot, inner = start // B, pl.multiple_of(start % B, width)

    def rows_of(d):
        return pl.ds(pl.multiple_of(lax.rem(col_pos - d + grid_cols, grid_cols) * share, share), share)

    def product():
        for d in range(grid_cols):
            out_ref[rows_of(d), :] = prev_ref[rows_of(d), :] - dot(sides[d][...], col_ref[0])

    def panel():
        at = pl.multiple_of(col_pos * B + inner, width)
        for d in range(grid_cols):
            out_ref[rows_of(d), :] = sides[d][:, pl.ds(at, width)].astype(jnp.float32)
        step = col_pos + (FIRST if last else 0)

        @pl.when(row_pos == step)
        def _():
            out_ref[:B, :] = lower_ref[:, pl.ds(inner, width)]

        @pl.when(row_pos < step)
        def _():
            out_ref[:B, :] = jnp.zeros((B, width), jnp.float32)

    if last:
        in_panel = (slot == 1) & (col_pos + FIRST < STEPS)
        pl.when(in_panel)(panel)

        @pl.when(jnp.logical_not(in_panel))
        def _():
            product()

            @pl.when(row_pos < STEPS)
            def _():
                out_ref[:B, :] = jnp.zeros((B, width), jnp.float32)

    else:
        pl.when(slot == 0)(panel)

        @pl.when(slot > 0)
        def _():
            product()
            offset = slot * grid_cols + col_pos - row_pos
            level = offset // grid_rows

            @pl.when((offset >= 0) & (lax.rem(offset, grid_rows) == 0) & (level < slots))
            def _():
                own = pl.ds(pl.multiple_of(level * B, B), B)
                same = lax.broadcasted_iota(jnp.int32, (B, width), 0) == (
                    lax.broadcasted_iota(jnp.int32, (B, width), 1) + inner
                )
                value = nugget_ref[level, :, pl.ds(inner, width)]
                out_ref[own, :] += jnp.where(same, value, 0.0)


def trail(place, prev, sides, cols, lower, nugget, last, grid_rows, grid_cols):
    rows_here, cols_here = prev.shape
    share, depth = sides[0].shape
    width = min(B, share)
    slots = rows_here // B
    group = grid_rows // grid_cols
    skip = B // width if last else 0

    def col_block(u, place):
        start = (u + skip) * width
        slot, inner = start // B, start % B
        at = slot // group * B + inner
        return (slot % group * grid_cols + at // share, 0, at % share // width)

    def own_block(u, place):
        return (0, u + skip)

    block = pl.BlockSpec((rows_here, width), own_block)
    side = pl.BlockSpec((share, depth), lambda u, place: (0, 0))
    return pl.pallas_call(
        functools.partial(trail_body, last, grid_rows, grid_cols, slots, width),
        out_shape=jax.ShapeDtypeStruct(prev.shape, jnp.float32),
        grid_spec=pltpu.PrefetchScalarGridSpec(
            num_scalar_prefetch=1,
            grid=(cols_here // width - skip,),
            in_specs=[block]
            + [side] * grid_cols
            + [
                pl.BlockSpec((1, depth, width), col_block),
                pl.BlockSpec((B, B), lambda u, place: (0, 0)),
                pl.BlockSpec((slots, 1, B), lambda u, place: (0, 0, 0)),
            ],
            out_specs=block,
        ),
        input_output_aliases={1: 0} if last else {},
        compiler_params=pltpu.CompilerParams(
            vmem_limit_bytes=VMEM_LIMIT, dimension_semantics=("arbitrary",)
        ),
        cost_estimate=pl.CostEstimate(
            flops=2 * rows_here * cols_here * depth,
            bytes_accessed=8 * rows_here * cols_here,
            transcendentals=0,
        ),
        name="trail",
    )(place, prev, *sides, cols, lower, nugget)


def body(kernel, nugget):
    rows_here, cols_here = kernel.shape
    grid_rows = lax.axis_size("row")
    grid_cols = lax.axis_size("col")
    row_pos = lax.axis_index("row")
    col_pos = lax.axis_index("col")
    group = grid_rows // grid_cols
    share = rows_here // grid_cols
    slots = rows_here // B
    axes = ("row", "col")
    place = jnp.stack([row_pos, col_pos]).astype(jnp.int32)

    sent = assign_tiles(grid_cols)
    picked = [[0] * grid_cols for _ in range(grid_rows)]
    for row, col, slot, _ in sent.values():
        picked[row][col] = slot if row < STEPS else 0
    near, far = kernel[:B, :B], kernel[:B, B : 2 * B]
    passed = lax.ppermute(
        far,
        axes,
        [(a * grid_cols + a % grid_cols, STEPS * grid_cols + a % grid_cols) for a in range(STEPS - grid_cols)],
    )
    pick = jnp.asarray(picked, jnp.int32)[row_pos, col_pos]
    mine = jnp.where(row_pos == STEPS, passed, jnp.where(pick == 1, far, near))
    on_diagonal = (row_pos < STEPS) & (row_pos == pick * grid_cols + col_pos)
    same = jnp.arange(B)[:, None] == jnp.arange(B)[None, :]
    mine = mine + jnp.where(on_diagonal & same, nugget[:B][:, None], jnp.float32(0.0))
    tiles = lax.all_gather(mine, axes, axis=0, tiled=False)[: (STEPS + 1) * grid_cols]
    tiles_of = {pair: (row * grid_cols + col, turned) for pair, (row, col, _, turned) in sent.items()}

    top = jnp.transpose(kernel[:B].reshape(B, slots, group, B), (2, 0, 1, 3))
    top = jnp.transpose(top.reshape(group, B, grid_cols, share), (0, 2, 1, 3)).reshape(grid_rows, B, share)
    wide = lax.all_to_all(top, "row", split_axis=0, concat_axis=0, tiled=True)

    def exchange(col_own, row_own):
        cols = lax.all_gather(col_own, "row", axis=0, tiled=False)
        sides = []
        for d in range(grid_cols):
            pairs = []
            for g in range(group):
                for c in range(grid_cols):
                    for q in range(grid_cols):
                        source = (g * grid_cols + c) * grid_cols + q
                        target = (g * grid_cols + q) * grid_cols + (c + d) % grid_cols
                        pairs.append((source, target))
            sides.append(lax.ppermute(row_own, axes, pairs))
        return sides, cols

    nugget_rows = nugget.reshape(slots, 1, B)
    rest, col_own, row_own, lower = factor_group((tiles, wide), tiles_of, STEPS, FIRST, share)
    sides, cols = exchange(col_own, row_own)
    col_own, row_own, lower_late = factor_group((rest,), None, STEPS - FIRST, STEPS - FIRST, share)
    sides_late, cols_late = exchange(col_own, row_own)
    at = lax.dynamic_index_in_dim(lower, col_pos, 0, keepdims=False)
    matrix = trail(place, kernel, sides, cols, at, nugget_rows, False, grid_rows, grid_cols)
    at = lax.dynamic_index_in_dim(lower_late, jnp.minimum(col_pos, STEPS - FIRST - 1), 0, keepdims=False)
    return trail(place, matrix, sides_late, cols_late, at, nugget_rows, True, grid_rows, grid_cols)


def solution(mesh):
    return jax.shard_map(
        body,
        mesh=mesh,
        in_specs=(P("row", "col"), P("row")),
        out_specs=P("row", "col"),
        check_vma=False,
    )
```

```python
import functools

import jax
import jax.numpy as jnp
from jax import lax
from jax.experimental import pallas as pl
from jax.experimental.pallas import tpu as pltpu
from jax.sharding import PartitionSpec as P

B = 256
STEPS = 7
FIRST = 4
GROUPS = (2, 2, 2, 1)
STEP_COST = 100 * 10**9
SUB = 64
VMEM_LIMIT = 56 * 1024 * 1024


def assign_tiles(grid_cols):
    spare = STEPS
    sent, taken = {}, {}
    options = {}
    for a in range(STEPS):
        for b in range(a, STEPS):
            if b == a + grid_cols:
                sent[(a, b)] = (spare, a % grid_cols, 1, False)
                continue
            options[(a, b)] = [(a, b % grid_cols, b // grid_cols, False)]
            if a != b:
                options[(a, b)].append((b, a % grid_cols, a // grid_cols, True))

    def place(pair, seen):
        for option in options[pair]:
            device = option[:2]
            if device in seen:
                continue
            seen.add(device)
            if device not in taken or place(taken[device], seen):
                taken[device] = pair
                sent[pair] = option
                return True
        return False

    for pair in options:
        assert place(pair, set())
    return sent


def split(x):
    hi = x.astype(jnp.bfloat16)
    return hi, (x - hi.astype(jnp.float32)).astype(jnp.bfloat16)


def dot(a, b, dims=(1, 0)):
    return lax.dot_general(a, b, (((dims[0],), (dims[1],)), ((), ())), preferred_element_type=jnp.float32)


def dot_wide(a, b, dims=(1, 0)):
    a_hi, a_lo = split(a)
    b_hi, b_lo = split(b)
    return dot(a_hi, b_hi, dims) + (dot(a_hi, b_lo, dims) + dot(a_lo, b_hi, dims))


def eliminate(block):
    width = block.shape[1]
    count = SUB // 8
    rows = [block[8 * v : 8 * v + 8] for v in range(count)]
    sublane = lax.broadcasted_iota(jnp.int32, (8, width), 0)

    def lane(x, at):
        return jnp.broadcast_to(x[:, at : at + 1], (8, width))

    def row(x, at):
        return jnp.broadcast_to(x[at : at + 1], (8, width))

    for g in range(count):
        cols = [[lane(rows[v], 8 * g + m) for v in range(g, count)] for m in range(8)]
        pivot = {(a, b): row(cols[b][0], a) for b in range(8) for a in range(b, 8)}
        root, low = [None] * 8, {}
        for b in range(8):
            root[b] = lax.rsqrt(pivot[b, b])
            for a in range(b + 1, 8):
                low[a, b] = pivot[a, b] * root[b]
            for a in range(b + 1, 8):
                for c in range(b + 1, a + 1):
                    pivot[a, c] = pivot[a, c] - low[a, b] * low[c, b]
        inv = {}
        for b in range(8):
            inv[b, b] = root[b]
            for a in range(b + 1, 8):
                total = low[a, b] * inv[b, b]
                for m in range(b + 1, a):
                    total = total + low[a, m] * inv[m, b]
                inv[a, b] = -root[a] * total
        solved = None
        for b in range(8):
            coef = jnp.zeros((8, width), jnp.float32)
            for a in range(b, 8):
                coef = jnp.where(sublane == a, inv[a, b], coef)
            term = coef * row(rows[g], b)
            solved = term if solved is None else solved + term
        rows[g] = solved
        if g + 1 < count:
            across = [row(solved, m) for m in range(8)]
            for v in range(g + 1, count):
                total = None
                for m in range(8):
                    factor = inv[m, 0] * cols[0][v - g]
                    for b in range(1, m + 1):
                        factor = factor + inv[m, b] * cols[b][v - g]
                    term = factor * across[m]
                    total = term if total is None else total + term
                rows[v] = rows[v] - total
    return jnp.concatenate(rows, axis=0)


def factor_tile(work):
    eye = (
        lax.broadcasted_iota(jnp.int32, (SUB, 2 * SUB), 0) + SUB
        == lax.broadcasted_iota(jnp.int32, (SUB, 2 * SUB), 1)
    ).astype(jnp.float32)
    left = lax.broadcasted_iota(jnp.int32, (SUB, 2 * SUB), 1) < SUB
    for b in range(B // SUB):
        at = b * SUB
        base = at // (2 * SUB) * (2 * SUB)
        odd = at != base
        pair = work[at : at + SUB, base : base + 2 * SUB]
        if odd:
            pair = pltpu.roll(pair, SUB, 1)
        done = eliminate(jnp.where(left, pair, eye))
        moved = pltpu.roll(done, SUB, 1)
        inverse = moved[:, :SUB]
        end = B + base + 2 * SUB
        solved = dot_wide(inverse, work[at : at + SUB, base:end])
        if at + SUB < B:
            padded = jnp.where(left, 0.0, done) if odd else jnp.where(left, moved, 0.0)
            below = dot_wide(work[at + SUB : B, base : base + 2 * SUB], padded, (1, 1))
            start = (at + SUB) // (2 * SUB) * (2 * SUB)
            work[at + SUB : B, start:end] -= dot_wide(below, solved[:, start - base :])
        work[at : at + SUB, base:end] = solved


def read_tile(tile, turned):
    return tile.T if turned else tile


def factor_steps(held, panel, work, count, steps, stop, chunk, lower_ref, after):
    above = lax.broadcasted_iota(jnp.int32, (B, B), 0)
    beside = lax.broadcasted_iota(jnp.int32, (B, B), 1)

    def step(k, carry):
        at = pl.multiple_of(k * B, B)
        work[:, :B] = held[k, :, pl.ds(at, B)]
        work[:, B:] = (above == beside).astype(jnp.float32)
        factor_tile(work)
        lower_ref[k] = jnp.where(above >= beside, work[:, :B].T, 0.0)
        inv_hi, inv_lo = split(work[:, B:])

        def solve(c, carry):
            where = pl.ds(pl.multiple_of(c * chunk, chunk), chunk)
            hi, lo = split(held[k, :, where])
            panel[:, where] = (dot(inv_hi, hi) + (dot(inv_hi, lo) + dot(inv_lo, hi))).astype(jnp.bfloat16)
            return carry

        lax.fori_loop((k + 1) * (B // chunk), stop // chunk, solve, 0)
        after(k, at)

        def reduce(i, carry):
            side = panel[:, pl.ds(pl.multiple_of(i * B, B), B)].T
            held[i] -= dot(side, panel[...])
            return carry

        lax.fori_loop(k + 1, count, reduce, 0)
        return carry

    panel[...] = jnp.zeros_like(panel)
    lax.fori_loop(0, steps, step, 0)


def open_body(tiles_of, steps, tiles_ref, rest_ref, panel_ref, inverse_ref, lower_ref, held, panel, work):
    for (a, b), (index, turned) in tiles_of.items():
        held[a, :, b * B : (b + 1) * B] = read_tile(tiles_ref[index], turned)

    def after(k, at):
        panel_ref[k] = panel[...]
        inverse_ref[k] = work[:, B:]

    factor_steps(held, panel, work, STEPS, steps, STEPS * B, B, lower_ref, after)
    rest_ref[...] = held[steps:, :, steps * B :]


def open_group(tiles, tiles_of, steps):
    f32, bf16 = jnp.float32, jnp.bfloat16
    whole = pl.BlockSpec(memory_space=pltpu.VMEM)
    left = STEPS - steps
    return pl.pallas_call(
        functools.partial(open_body, tiles_of, steps),
        out_shape=[
            jax.ShapeDtypeStruct((left, B, left * B), f32),
            jax.ShapeDtypeStruct((steps, B, STEPS * B), bf16),
            jax.ShapeDtypeStruct((steps, B, B), f32),
            jax.ShapeDtypeStruct((steps, B, B), f32),
        ],
        in_specs=[whole],
        out_specs=[whole] * 4,
        scratch_shapes=[
            pltpu.VMEM((STEPS, B, STEPS * B), f32),
            pltpu.VMEM((B, STEPS * B), bf16),
            pltpu.VMEM((B, 2 * B), f32),
        ],
        compiler_params=pltpu.CompilerParams(vmem_limit_bytes=VMEM_LIMIT),
        cost_estimate=pl.CostEstimate(flops=steps * STEP_COST, bytes_accessed=2**24, transcendentals=0),
        name="open_diagonal",
    )(tiles)


def solve_body(grid_rows, steps, place, *refs):
    wide_refs = refs[:grid_rows]
    panel_ref, inverse_ref, rest_ref, col_ref, row_ref, held = refs[grid_rows:]
    for r in range(grid_rows):
        held[place[0] ^ r] = wide_refs[r][...]
    for k in range(steps):
        own = dot_wide(inverse_ref[k], held[k]).astype(jnp.bfloat16)
        col_ref[k * B : (k + 1) * B, :] = own
        row_ref[:, k * B : (k + 1) * B] = own.T

        def reduce(i, carry):
            side = panel_ref[k, :, pl.ds(pl.multiple_of(i * B, B), B)].T
            held[i] -= dot(side, own)
            return carry

        lax.fori_loop(k + 1, STEPS, reduce, 0)
    rest_ref[...] = held[steps:STEPS]


def solve_group(place, wide, panels, inverse, steps):
    share = wide[0].shape[1]
    f32, bf16 = jnp.float32, jnp.bfloat16
    whole = pl.BlockSpec(memory_space=pltpu.VMEM)
    return pl.pallas_call(
        functools.partial(solve_body, len(wide), steps),
        out_shape=[
            jax.ShapeDtypeStruct((STEPS - steps, B, share), f32),
            jax.ShapeDtypeStruct((steps * B, share), bf16),
            jax.ShapeDtypeStruct((share, steps * B), bf16),
        ],
        in_specs=[pl.BlockSpec(memory_space=pltpu.SMEM)] + [whole] * (len(wide) + 2),
        out_specs=[whole] * 3,
        scratch_shapes=[pltpu.VMEM((len(wide), B, share), f32)],
        compiler_params=pltpu.CompilerParams(vmem_limit_bytes=VMEM_LIMIT),
        cost_estimate=pl.CostEstimate(flops=10**9, bytes_accessed=2**24, transcendentals=0),
        name="solve_rows",
    )(place, *wide, panels, inverse)


def factor_body(count, steps, share, chunk, waited, diag_ref, wide_ref, *refs):
    refs = refs[waited:]
    if steps < count:
        rest_ref, rest_wide_ref, *refs = refs
    col_ref, row_ref, lower_ref, held, panel, work = refs
    edge = count * B
    held[:, :, :edge] = diag_ref[...]
    held[:, :, edge:] = wide_ref[...]

    def after(k, at):
        own = panel[:, edge:]
        col_ref[pl.ds(at, B), :] = own
        row_ref[:, pl.ds(at, B)] = own.T

    factor_steps(held, panel, work, count, steps, edge + share, chunk, lower_ref, after)
    if steps < count:
        rest_ref[...] = held[steps:, :, steps * B : edge]
        rest_wide_ref[...] = held[steps:, :, edge:]


def factor_group(diag, wide, steps, waited):
    count, _, share = wide.shape
    f32, bf16 = jnp.float32, jnp.bfloat16
    outs = [
        jax.ShapeDtypeStruct((steps * B, share), bf16),
        jax.ShapeDtypeStruct((share, steps * B), bf16),
        jax.ShapeDtypeStruct((steps, B, B), f32),
    ]
    left = count - steps
    if left:
        outs = [
            jax.ShapeDtypeStruct((left, B, left * B), f32),
            jax.ShapeDtypeStruct((left, B, share), f32),
        ] + outs
    whole = pl.BlockSpec(memory_space=pltpu.VMEM)
    return pl.pallas_call(
        functools.partial(factor_body, count, steps, share, min(B, share), len(waited)),
        out_shape=outs,
        in_specs=[whole, whole] + [pl.BlockSpec(memory_space=pl.ANY)] * len(waited),
        out_specs=[whole] * len(outs),
        scratch_shapes=[
            pltpu.VMEM((count, B, count * B + share), f32),
            pltpu.VMEM((B, count * B + share), bf16),
            pltpu.VMEM((B, 2 * B), f32),
        ],
        compiler_params=pltpu.CompilerParams(vmem_limit_bytes=VMEM_LIMIT),
        cost_estimate=pl.CostEstimate(flops=steps * STEP_COST, bytes_accessed=2**24, transcendentals=0),
        name="factor",
    )(diag, wide, *waited)


def pack_body(place, kernel_ref, out_ref):
    out_ref[0] = kernel_ref[...]


def pack(place, kernel, grid_rows, grid_cols, share):
    group = grid_rows // grid_cols
    width = min(B, share)

    def source(r, j, place):
        chunk = place[0] ^ r
        at = chunk % grid_cols * share + j * width
        return (0, ((at // B * group + chunk // grid_cols) * B + at % B) // width)

    return pl.pallas_call(
        pack_body,
        out_shape=jax.ShapeDtypeStruct((grid_rows, B, share), jnp.float32),
        grid_spec=pltpu.PrefetchScalarGridSpec(
            num_scalar_prefetch=1,
            grid=(grid_rows, share // width),
            in_specs=[pl.BlockSpec((B, width), source)],
            out_specs=pl.BlockSpec((1, B, width), lambda r, j, place: (r, 0, j)),
        ),
        cost_estimate=pl.CostEstimate(flops=0, bytes_accessed=2**23, transcendentals=0),
        name="pack",
    )(place, kernel)


def trail_body(last, parts, grid_rows, grid_cols, slots, width, *refs):
    place, prev_ref, *sides = refs[: 2 + parts * grid_cols]
    col_refs = refs[2 + parts * grid_cols : 2 + parts * (grid_cols + 1)]
    lower_ref, nugget_ref = refs[2 + parts * (grid_cols + 1) :][:2]
    out_ref = refs[-1]
    sides = [sides[n * grid_cols : (n + 1) * grid_cols] for n in range(parts)]
    row_pos, col_pos = place[0], place[1]
    share = sides[0][0].shape[0]
    skip = B // width if last else 0
    start = (pl.program_id(0) + skip) * width
    slot, inner = start // B, pl.multiple_of(start % B, width)

    def rows_of(d):
        return pl.ds(pl.multiple_of(lax.rem(col_pos - d + grid_cols, grid_cols) * share, share), share)

    def product():
        for d in range(grid_cols):
            total = dot(sides[0][d][...], col_refs[0][0])
            for n in range(1, parts):
                total = total + dot(sides[n][d][...], col_refs[n][0])
            out_ref[rows_of(d), :] = prev_ref[rows_of(d), :] - total

    def panel():
        first = 0
        for n in range(parts):
            wide = sides[n][0].shape[1] // B

            @pl.when((col_pos >= first) & (col_pos < first + wide))
            def _():
                at = pl.multiple_of((col_pos - first) * B + inner, width)
                for d in range(grid_cols):
                    out_ref[rows_of(d), :] = sides[n][d][:, pl.ds(at, width)].astype(jnp.float32)

            first += wide
        step = col_pos + (FIRST if last else 0)

        @pl.when(row_pos == step)
        def _():
            out_ref[:B, :] = lower_ref[:, pl.ds(inner, width)]

        @pl.when(row_pos < step)
        def _():
            out_ref[:B, :] = jnp.zeros((B, width), jnp.float32)

    if last:
        in_panel = (slot == 1) & (col_pos + FIRST < STEPS)
        pl.when(in_panel)(panel)

        @pl.when(jnp.logical_not(in_panel))
        def _():
            product()

            @pl.when(row_pos < STEPS)
            def _():
                out_ref[:B, :] = jnp.zeros((B, width), jnp.float32)

    else:
        pl.when(slot == 0)(panel)

        @pl.when(slot > 0)
        def _():
            product()
            offset = slot * grid_cols + col_pos - row_pos
            level = offset // grid_rows

            @pl.when((offset >= 0) & (lax.rem(offset, grid_rows) == 0) & (level < slots))
            def _():
                own = pl.ds(pl.multiple_of(level * B, B), B)
                same = lax.broadcasted_iota(jnp.int32, (B, width), 0) == (
                    lax.broadcasted_iota(jnp.int32, (B, width), 1) + inner
                )
                value = nugget_ref[level, :, pl.ds(inner, width)]
                out_ref[own, :] += jnp.where(same, value, 0.0)


def trail(place, prev, sides, cols, lower, nugget, last, grid_rows, grid_cols):
    rows_here, cols_here = prev.shape
    share = sides[0][0].shape[0]
    depths = [part[0].shape[1] for part in sides]
    width = min(B, share)
    slots = rows_here // B
    group = grid_rows // grid_cols
    skip = B // width if last else 0

    def col_block(u, place):
        start = (u + skip) * width
        slot, inner = start // B, start % B
        at = slot // group * B + inner
        return (slot % group * grid_cols + at // share, 0, at % share // width)

    def own_block(u, place):
        return (0, u + skip)

    block = pl.BlockSpec((rows_here, width), own_block)
    return pl.pallas_call(
        functools.partial(trail_body, last, len(sides), grid_rows, grid_cols, slots, width),
        out_shape=jax.ShapeDtypeStruct(prev.shape, jnp.float32),
        grid_spec=pltpu.PrefetchScalarGridSpec(
            num_scalar_prefetch=1,
            grid=(cols_here // width - skip,),
            in_specs=[block]
            + [pl.BlockSpec((share, depth), lambda u, place: (0, 0)) for depth in depths for _ in range(grid_cols)]
            + [pl.BlockSpec((1, depth, width), col_block) for depth in depths]
            + [
                pl.BlockSpec((B, B), lambda u, place: (0, 0)),
                pl.BlockSpec((slots, 1, B), lambda u, place: (0, 0, 0)),
            ],
            out_specs=block,
        ),
        input_output_aliases={1: 0} if last else {},
        compiler_params=pltpu.CompilerParams(
            vmem_limit_bytes=VMEM_LIMIT, dimension_semantics=("arbitrary",)
        ),
        cost_estimate=pl.CostEstimate(
            flops=2 * rows_here * cols_here * sum(depths),
            bytes_accessed=8 * rows_here * cols_here,
            transcendentals=0,
        ),
        name="trail",
    )(place, prev, *[x for part in sides for x in part], *cols, lower, nugget)


def body(kernel, nugget):
    rows_here, cols_here = kernel.shape
    grid_rows = lax.axis_size("row")
    grid_cols = lax.axis_size("col")
    row_pos = lax.axis_index("row")
    col_pos = lax.axis_index("col")
    group = grid_rows // grid_cols
    share = rows_here // grid_cols
    slots = rows_here // B
    axes = ("row", "col")
    place = jnp.stack([row_pos, col_pos]).astype(jnp.int32)

    sent = assign_tiles(grid_cols)
    picked = [[0] * grid_cols for _ in range(grid_rows)]
    for row, col, slot, _ in sent.values():
        picked[row][col] = slot if row < STEPS else 0
    near, far = kernel[:B, :B], kernel[:B, B : 2 * B]
    passed = lax.ppermute(
        far,
        axes,
        [(a * grid_cols + a % grid_cols, STEPS * grid_cols + a % grid_cols) for a in range(STEPS - grid_cols)],
    )
    pick = jnp.asarray(picked, jnp.int32)[row_pos, col_pos]
    mine = jnp.where(row_pos == STEPS, passed, jnp.where(pick == 1, far, near))
    on_diagonal = (row_pos < STEPS) & (row_pos == pick * grid_cols + col_pos)
    same = jnp.arange(B)[:, None] == jnp.arange(B)[None, :]
    mine = mine + jnp.where(on_diagonal & same, nugget[:B][:, None], jnp.float32(0.0))
    tiles = lax.all_gather(mine, axes, axis=0, tiled=False)[: (STEPS + 1) * grid_cols]
    tiles_of = {pair: (row * grid_cols + col, turned) for pair, (row, col, _, turned) in sent.items()}

    packed = pack(place, kernel, grid_rows, grid_cols, share)
    wide = [packed[0]]
    for r in range(1, grid_rows):
        pairs = [
            (p * grid_cols + q, (p ^ r) * grid_cols + q) for p in range(STEPS) for q in range(grid_cols)
        ]
        wide.append(lax.ppermute(packed[r], axes, pairs))

    def exchange(col_own, row_own):
        cols = lax.all_gather(col_own, "row", axis=0, tiled=False)
        sides = []
        for d in range(grid_cols):
            pairs = []
            for g in range(group):
                for c in range(grid_cols):
                    for q in range(grid_cols):
                        source = (g * grid_cols + c) * grid_cols + q
                        target = (g * grid_cols + q) * grid_cols + (c + d) % grid_cols
                        pairs.append((source, target))
            sides.append(lax.ppermute(row_own, axes, pairs))
        return sides, cols

    nugget_rows = nugget.reshape(slots, 1, B)
    sides, cols, lowers = [], [], []

    def send(col_own, row_own):
        side, col = exchange(col_own, row_own)
        sides.append(side)
        cols.append(col)

    diag, panels, inverse, lower = open_group(tiles, tiles_of, GROUPS[0])
    lowers.append(lower)
    rest, col_own, row_own = solve_group(place, wide, panels, inverse, GROUPS[0])
    send(col_own, row_own)
    for n in range(1, len(GROUPS)):
        made = factor_group(diag, rest, GROUPS[n], [*sides[n - 2], cols[n - 2]] if n >= 2 else [])
        if n + 1 < len(GROUPS):
            diag, rest, *made = made
        col_own, row_own, lower = made
        lowers.append(lower)
        send(col_own, row_own)
    lower = jnp.concatenate(lowers)
    at = lax.dynamic_index_in_dim(lower, col_pos, 0, keepdims=False)
    matrix = trail(place, kernel, sides[:2], cols[:2], at, nugget_rows, False, grid_rows, grid_cols)
    at = lax.dynamic_index_in_dim(lower, jnp.minimum(col_pos + FIRST, STEPS - 1), 0, keepdims=False)
    return trail(place, matrix, sides[2:], cols[2:], at, nugget_rows, True, grid_rows, grid_cols)


def solution(mesh):
    return jax.shard_map(
        body,
        mesh=mesh,
        in_specs=(P("row", "col"), P("row")),
        out_specs=P("row", "col"),
        check_vma=False,
    )
```

```python
import functools

import jax
import jax.numpy as jnp
from jax import lax
from jax.experimental import pallas as pl
from jax.experimental.pallas import tpu as pltpu
from jax.sharding import PartitionSpec as P

B = 256
STEPS = 7
FIRST = 4
GROUPS = (2, 2, 2, 1)
STEP_COST = 100 * 10**9
SUB = 64
VMEM_LIMIT = 56 * 1024 * 1024


def assign_tiles(grid_cols):
    spare = STEPS
    sent, taken = {}, {}
    options = {}
    for a in range(STEPS):
        for b in range(a, STEPS):
            if b == a + grid_cols:
                sent[(a, b)] = (spare, a % grid_cols, 1, False)
                continue
            options[(a, b)] = [(a, b % grid_cols, b // grid_cols, False)]
            if a != b:
                options[(a, b)].append((b, a % grid_cols, a // grid_cols, True))

    def place(pair, seen):
        for option in options[pair]:
            device = option[:2]
            if device in seen:
                continue
            seen.add(device)
            if device not in taken or place(taken[device], seen):
                taken[device] = pair
                sent[pair] = option
                return True
        return False

    for pair in options:
        assert place(pair, set())
    return sent


def split(x):
    hi = x.astype(jnp.bfloat16)
    return hi, (x - hi.astype(jnp.float32)).astype(jnp.bfloat16)


def dot(a, b, dims=(1, 0)):
    return lax.dot_general(a, b, (((dims[0],), (dims[1],)), ((), ())), preferred_element_type=jnp.float32)


def dot_wide(a, b, dims=(1, 0)):
    a_hi, a_lo = split(a)
    b_hi, b_lo = split(b)
    return dot(a_hi, b_hi, dims) + (dot(a_hi, b_lo, dims) + dot(a_lo, b_hi, dims))


def eliminate(block):
    width = block.shape[1]
    count = SUB // 8
    rows = [block[8 * v : 8 * v + 8] for v in range(count)]
    sublane = lax.broadcasted_iota(jnp.int32, (8, width), 0)

    def lane(x, at):
        return jnp.broadcast_to(x[:, at : at + 1], (8, width))

    def row(x, at):
        return jnp.broadcast_to(x[at : at + 1], (8, width))

    for g in range(count):
        cols = [[lane(rows[v], 8 * g + m) for v in range(g, count)] for m in range(8)]
        pivot = {(a, b): row(cols[b][0], a) for b in range(8) for a in range(b, 8)}
        root, low = [None] * 8, {}
        for b in range(8):
            root[b] = lax.rsqrt(pivot[b, b])
            for a in range(b + 1, 8):
                low[a, b] = pivot[a, b] * root[b]
            for a in range(b + 1, 8):
                for c in range(b + 1, a + 1):
                    pivot[a, c] = pivot[a, c] - low[a, b] * low[c, b]
        inv = {}
        for b in range(8):
            inv[b, b] = root[b]
            for a in range(b + 1, 8):
                total = low[a, b] * inv[b, b]
                for m in range(b + 1, a):
                    total = total + low[a, m] * inv[m, b]
                inv[a, b] = -root[a] * total
        solved = None
        for b in range(8):
            coef = jnp.zeros((8, width), jnp.float32)
            for a in range(b, 8):
                coef = jnp.where(sublane == a, inv[a, b], coef)
            term = coef * row(rows[g], b)
            solved = term if solved is None else solved + term
        rows[g] = solved
        if g + 1 < count:
            across = [row(solved, m) for m in range(8)]
            for v in range(g + 1, count):
                total = None
                for m in range(8):
                    factor = inv[m, 0] * cols[0][v - g]
                    for b in range(1, m + 1):
                        factor = factor + inv[m, b] * cols[b][v - g]
                    term = factor * across[m]
                    total = term if total is None else total + term
                rows[v] = rows[v] - total
    return jnp.concatenate(rows, axis=0)


def factor_tile(work):
    eye = (
        lax.broadcasted_iota(jnp.int32, (SUB, 2 * SUB), 0) + SUB
        == lax.broadcasted_iota(jnp.int32, (SUB, 2 * SUB), 1)
    ).astype(jnp.float32)
    left = lax.broadcasted_iota(jnp.int32, (SUB, 2 * SUB), 1) < SUB
    for b in range(B // SUB):
        at = b * SUB
        base = at // (2 * SUB) * (2 * SUB)
        odd = at != base
        pair = work[at : at + SUB, base : base + 2 * SUB]
        if odd:
            pair = pltpu.roll(pair, SUB, 1)
        done = eliminate(jnp.where(left, pair, eye))
        moved = pltpu.roll(done, SUB, 1)
        inverse = moved[:, :SUB]
        end = B + base + 2 * SUB
        solved = dot_wide(inverse, work[at : at + SUB, base:end])
        if at + SUB < B:
            padded = jnp.where(left, 0.0, done) if odd else jnp.where(left, moved, 0.0)
            below = dot_wide(work[at + SUB : B, base : base + 2 * SUB], padded, (1, 1))
            start = (at + SUB) // (2 * SUB) * (2 * SUB)
            work[at + SUB : B, start:end] -= dot_wide(below, solved[:, start - base :])
        work[at : at + SUB, base:end] = solved


def read_tile(tile, turned):
    tile = tile[:B].astype(jnp.float32)
    return tile.T if turned else tile


def read_diagonal(packed):
    above = lax.broadcasted_iota(jnp.int32, (B, B), 0)
    beside = lax.broadcasted_iota(jnp.int32, (B, B), 1)
    packed = packed.astype(jnp.float32)
    tile = packed[:B]
    below = jnp.where(above > beside, tile + tile.T, 0.0)
    middle = jnp.where(above == beside, tile + packed[B : B + 1], 0.0)
    return below + below.T + middle


def factor_steps(held, panel, work, count, steps, stop, chunk, lower_ref, after):
    above = lax.broadcasted_iota(jnp.int32, (B, B), 0)
    beside = lax.broadcasted_iota(jnp.int32, (B, B), 1)

    def step(k, carry):
        at = pl.multiple_of(k * B, B)
        work[:, :B] = held[k, :, pl.ds(at, B)]
        work[:, B:] = (above == beside).astype(jnp.float32)
        factor_tile(work)
        lower_ref[k] = jnp.where(above >= beside, work[:, :B].T, 0.0)
        inv_hi, inv_lo = split(work[:, B:])

        def solve(c, carry):
            where = pl.ds(pl.multiple_of(c * chunk, chunk), chunk)
            hi, lo = split(held[k, :, where])
            panel[:, where] = (dot(inv_hi, hi) + (dot(inv_hi, lo) + dot(inv_lo, hi))).astype(jnp.bfloat16)
            return carry

        lax.fori_loop((k + 1) * (B // chunk), stop // chunk, solve, 0)
        after(k, at)

        def reduce(i, carry):
            side = panel[:, pl.ds(pl.multiple_of(i * B, B), B)].T
            held[i] -= dot(side, panel[...])
            return carry

        lax.fori_loop(k + 1, count, reduce, 0)
        return carry

    panel[...] = jnp.zeros_like(panel)
    lax.fori_loop(0, steps, step, 0)


def open_body(tiles_of, steps, tiles_ref, rest_ref, panel_ref, inverse_ref, lower_ref, held, panel, work):
    for (a, b), (index, turned) in tiles_of.items():
        tile = read_diagonal(tiles_ref[index]) if a == b else read_tile(tiles_ref[index], turned)
        held[a, :, b * B : (b + 1) * B] = tile

    def after(k, at):
        panel_ref[k] = panel[...]
        inverse_ref[k] = work[:, B:]

    factor_steps(held, panel, work, STEPS, steps, STEPS * B, B, lower_ref, after)
    rest_ref[...] = held[steps:, :, steps * B :]


def open_group(tiles, tiles_of, steps):
    f32, bf16 = jnp.float32, jnp.bfloat16
    whole = pl.BlockSpec(memory_space=pltpu.VMEM)
    left = STEPS - steps
    return pl.pallas_call(
        functools.partial(open_body, tiles_of, steps),
        out_shape=[
            jax.ShapeDtypeStruct((left, B, left * B), f32),
            jax.ShapeDtypeStruct((steps, B, STEPS * B), bf16),
            jax.ShapeDtypeStruct((steps, B, B), f32),
            jax.ShapeDtypeStruct((steps, B, B), f32),
        ],
        in_specs=[whole],
        out_specs=[whole] * 4,
        scratch_shapes=[
            pltpu.VMEM((STEPS, B, STEPS * B), f32),
            pltpu.VMEM((B, STEPS * B), bf16),
            pltpu.VMEM((B, 2 * B), f32),
        ],
        compiler_params=pltpu.CompilerParams(vmem_limit_bytes=VMEM_LIMIT),
        cost_estimate=pl.CostEstimate(flops=steps * STEP_COST, bytes_accessed=2**24, transcendentals=0),
        name="open_diagonal",
    )(tiles)


def solve_body(grid_rows, steps, place, *refs):
    wide_refs = refs[:grid_rows]
    panel_ref, inverse_ref, rest_ref, col_ref, row_ref, held = refs[grid_rows:]
    for r in range(grid_rows):
        held[place[0] ^ r] = wide_refs[r][...]
    for k in range(steps):
        own = dot_wide(inverse_ref[k], held[k]).astype(jnp.bfloat16)
        col_ref[k * B : (k + 1) * B, :] = own
        row_ref[:, k * B : (k + 1) * B] = own.T

        def reduce(i, carry):
            side = panel_ref[k, :, pl.ds(pl.multiple_of(i * B, B), B)].T
            held[i] -= dot(side, own)
            return carry

        lax.fori_loop(k + 1, STEPS, reduce, 0)
    rest_ref[...] = held[steps:STEPS]


def solve_group(place, wide, panels, inverse, steps):
    share = wide[0].shape[1]
    f32, bf16 = jnp.float32, jnp.bfloat16
    whole = pl.BlockSpec(memory_space=pltpu.VMEM)
    return pl.pallas_call(
        functools.partial(solve_body, len(wide), steps),
        out_shape=[
            jax.ShapeDtypeStruct((STEPS - steps, B, share), f32),
            jax.ShapeDtypeStruct((steps * B, share), bf16),
            jax.ShapeDtypeStruct((share, steps * B), bf16),
        ],
        in_specs=[pl.BlockSpec(memory_space=pltpu.SMEM)] + [whole] * (len(wide) + 2),
        out_specs=[whole] * 3,
        scratch_shapes=[pltpu.VMEM((len(wide), B, share), f32)],
        compiler_params=pltpu.CompilerParams(vmem_limit_bytes=VMEM_LIMIT),
        cost_estimate=pl.CostEstimate(flops=10**9, bytes_accessed=2**24, transcendentals=0),
        name="solve_rows",
    )(place, *wide, panels, inverse)


def factor_body(count, steps, share, chunk, earlier, waited, diag_ref, wide_ref, *refs):
    before, refs = refs[: 2 if earlier else 0], refs[(2 if earlier else 0) + waited :]
    if steps < count:
        rest_ref, rest_wide_ref, *refs = refs
    col_ref, row_ref, lower_ref, held, panel, work = refs
    edge = count * B
    held[:, :, :edge] = diag_ref[...]
    held[:, :, edge:] = wide_ref[...]
    if before:
        col_ref[:earlier, :] = before[0][...]
        row_ref[:, :earlier] = before[1][...]

    def after(k, at):
        own = panel[:, edge:]
        at = pl.multiple_of(at + earlier, B)
        col_ref[pl.ds(at, B), :] = own
        row_ref[:, pl.ds(at, B)] = own.T

    factor_steps(held, panel, work, count, steps, edge + share, chunk, lower_ref, after)
    if steps < count:
        rest_ref[...] = held[steps:, :, steps * B : edge]
        rest_wide_ref[...] = held[steps:, :, edge:]


def factor_group(diag, wide, steps, before, waited):
    count, _, share = wide.shape
    f32, bf16 = jnp.float32, jnp.bfloat16
    earlier = before[0].shape[0] if before else 0
    outs = [
        jax.ShapeDtypeStruct((earlier + steps * B, share), bf16),
        jax.ShapeDtypeStruct((share, earlier + steps * B), bf16),
        jax.ShapeDtypeStruct((steps, B, B), f32),
    ]
    left = count - steps
    if left:
        outs = [
            jax.ShapeDtypeStruct((left, B, left * B), f32),
            jax.ShapeDtypeStruct((left, B, share), f32),
        ] + outs
    whole = pl.BlockSpec(memory_space=pltpu.VMEM)
    return pl.pallas_call(
        functools.partial(factor_body, count, steps, share, min(B, share), earlier, len(waited)),
        out_shape=outs,
        in_specs=[whole] * (2 + len(before)) + [pl.BlockSpec(memory_space=pl.ANY)] * len(waited),
        out_specs=[whole] * len(outs),
        scratch_shapes=[
            pltpu.VMEM((count, B, count * B + share), f32),
            pltpu.VMEM((B, count * B + share), bf16),
            pltpu.VMEM((B, 2 * B), f32),
        ],
        compiler_params=pltpu.CompilerParams(vmem_limit_bytes=VMEM_LIMIT),
        cost_estimate=pl.CostEstimate(flops=steps * STEP_COST, bytes_accessed=2**24, transcendentals=0),
        name="factor",
    )(diag, wide, *before, *waited)


def pack_body(place, kernel_ref, out_ref):
    out_ref[0] = kernel_ref[...]


def pack(place, kernel, grid_rows, grid_cols, share):
    group = grid_rows // grid_cols
    width = min(B, share)

    def source(r, j, place):
        chunk = place[0] ^ r
        at = chunk % grid_cols * share + j * width
        return (0, ((at // B * group + chunk // grid_cols) * B + at % B) // width)

    return pl.pallas_call(
        pack_body,
        out_shape=jax.ShapeDtypeStruct((grid_rows, B, share), jnp.float32),
        grid_spec=pltpu.PrefetchScalarGridSpec(
            num_scalar_prefetch=1,
            grid=(grid_rows, share // width),
            in_specs=[pl.BlockSpec((B, width), source)],
            out_specs=pl.BlockSpec((1, B, width), lambda r, j, place: (r, 0, j)),
        ),
        cost_estimate=pl.CostEstimate(flops=0, bytes_accessed=2**23, transcendentals=0),
        name="pack",
    )(place, kernel)


def trail_body(last, parts, grid_rows, grid_cols, slots, width, *refs):
    place, prev_ref, *sides = refs[: 2 + parts * grid_cols]
    col_refs = refs[2 + parts * grid_cols : 2 + parts * (grid_cols + 1)]
    lower_ref, nugget_ref = refs[2 + parts * (grid_cols + 1) :][:2]
    out_ref = refs[-1]
    sides = [sides[n * grid_cols : (n + 1) * grid_cols] for n in range(parts)]
    row_pos, col_pos = place[0], place[1]
    share = sides[0][0].shape[0]
    skip = B // width if last else 0
    start = (pl.program_id(0) + skip) * width
    slot, inner = start // B, pl.multiple_of(start % B, width)

    def rows_of(d):
        return pl.ds(pl.multiple_of(lax.rem(col_pos - d + grid_cols, grid_cols) * share, share), share)

    def product():
        for d in range(grid_cols):
            total = dot(sides[0][d][...], col_refs[0][0])
            for n in range(1, parts):
                total = total + dot(sides[n][d][...], col_refs[n][0])
            out_ref[rows_of(d), :] = prev_ref[rows_of(d), :] - total

    def panel():
        first = 0
        for n in range(parts):
            wide = sides[n][0].shape[1] // B

            @pl.when((col_pos >= first) & (col_pos < first + wide))
            def _():
                at = pl.multiple_of((col_pos - first) * B + inner, width)
                for d in range(grid_cols):
                    out_ref[rows_of(d), :] = sides[n][d][:, pl.ds(at, width)].astype(jnp.float32)

            first += wide
        step = col_pos + (FIRST if last else 0)

        @pl.when(row_pos == step)
        def _():
            out_ref[:B, :] = lower_ref[:, pl.ds(inner, width)]

        @pl.when(row_pos < step)
        def _():
            out_ref[:B, :] = jnp.zeros((B, width), jnp.float32)

    if last:
        in_panel = (slot == 1) & (col_pos + FIRST < STEPS)
        pl.when(in_panel)(panel)

        @pl.when(jnp.logical_not(in_panel))
        def _():
            product()

            @pl.when(row_pos < STEPS)
            def _():
                out_ref[:B, :] = jnp.zeros((B, width), jnp.float32)

    else:
        pl.when(slot == 0)(panel)

        @pl.when(slot > 0)
        def _():
            product()
            offset = slot * grid_cols + col_pos - row_pos
            level = offset // grid_rows

            @pl.when((offset >= 0) & (lax.rem(offset, grid_rows) == 0) & (level < slots))
            def _():
                own = pl.ds(pl.multiple_of(level * B, B), B)
                same = lax.broadcasted_iota(jnp.int32, (B, width), 0) == (
                    lax.broadcasted_iota(jnp.int32, (B, width), 1) + inner
                )
                value = nugget_ref[level, :, pl.ds(inner, width)]
                out_ref[own, :] += jnp.where(same, value, 0.0)


def trail(place, prev, sides, cols, lower, nugget, last, grid_rows, grid_cols):
    rows_here, cols_here = prev.shape
    share = sides[0][0].shape[0]
    depths = [part[0].shape[1] for part in sides]
    width = min(B, share)
    slots = rows_here // B
    group = grid_rows // grid_cols
    skip = B // width if last else 0

    def col_block(u, place):
        start = (u + skip) * width
        slot, inner = start // B, start % B
        at = slot // group * B + inner
        return (slot % group * grid_cols + at // share, 0, at % share // width)

    def own_block(u, place):
        return (0, u + skip)

    block = pl.BlockSpec((rows_here, width), own_block)
    return pl.pallas_call(
        functools.partial(trail_body, last, len(sides), grid_rows, grid_cols, slots, width),
        out_shape=jax.ShapeDtypeStruct(prev.shape, jnp.float32),
        grid_spec=pltpu.PrefetchScalarGridSpec(
            num_scalar_prefetch=1,
            grid=(cols_here // width - skip,),
            in_specs=[block]
            + [pl.BlockSpec((share, depth), lambda u, place: (0, 0)) for depth in depths for _ in range(grid_cols)]
            + [pl.BlockSpec((1, depth, width), col_block) for depth in depths]
            + [
                pl.BlockSpec((B, B), lambda u, place: (0, 0)),
                pl.BlockSpec((slots, 1, B), lambda u, place: (0, 0, 0)),
            ],
            out_specs=block,
        ),
        input_output_aliases={1: 0} if last else {},
        compiler_params=pltpu.CompilerParams(
            vmem_limit_bytes=VMEM_LIMIT, dimension_semantics=("arbitrary",)
        ),
        cost_estimate=pl.CostEstimate(
            flops=2 * rows_here * cols_here * sum(depths),
            bytes_accessed=8 * rows_here * cols_here,
            transcendentals=0,
        ),
        name="trail",
    )(place, prev, *[x for part in sides for x in part], *cols, lower, nugget)


def body(kernel, nugget):
    rows_here, cols_here = kernel.shape
    grid_rows = lax.axis_size("row")
    grid_cols = lax.axis_size("col")
    row_pos = lax.axis_index("row")
    col_pos = lax.axis_index("col")
    group = grid_rows // grid_cols
    share = rows_here // grid_cols
    slots = rows_here // B
    axes = ("row", "col")
    place = jnp.stack([row_pos, col_pos]).astype(jnp.int32)

    sent = assign_tiles(grid_cols)
    picked = [[0] * grid_cols for _ in range(grid_rows)]
    for row, col, slot, _ in sent.values():
        picked[row][col] = slot if row < STEPS else 0
    near, far = kernel[:B, :B], kernel[:B, B : 2 * B]
    passed = lax.ppermute(
        far.astype(jnp.bfloat16),
        axes,
        [(a * grid_cols + a % grid_cols, STEPS * grid_cols + a % grid_cols) for a in range(STEPS - grid_cols)],
    )
    pick = jnp.asarray(picked, jnp.int32)[row_pos, col_pos]
    mine = jnp.where(pick == 1, far, near)
    on_diagonal = (row_pos < STEPS) & (row_pos == pick * grid_cols + col_pos)
    across, down = jnp.arange(B)[None, :], jnp.arange(B)[:, None]
    tile = mine + jnp.where(down == across, nugget[:B][:, None], jnp.float32(0.0))
    kept = lax.reduce_precision(tile, exponent_bits=8, mantissa_bits=7)
    remainder = tile - kept
    tile = jnp.where(down >= across, kept, remainder.T)
    middle = jnp.sum(jnp.where(down == across, remainder, 0.0), axis=0, keepdims=True)
    mine = jnp.where(on_diagonal, tile, mine).astype(jnp.bfloat16)
    mine = jnp.where(row_pos == STEPS, passed, mine)
    mine = jnp.concatenate([mine, jnp.broadcast_to(middle, (16, B)).astype(jnp.bfloat16)])
    tiles = lax.all_gather(mine, axes, axis=0, tiled=False)[: (STEPS + 1) * grid_cols]
    tiles_of = {pair: (row * grid_cols + col, turned) for pair, (row, col, _, turned) in sent.items()}

    packed = pack(place, kernel, grid_rows, grid_cols, share)
    wide = [packed[0]]
    for r in range(1, grid_rows):
        pairs = [
            (p * grid_cols + q, (p ^ r) * grid_cols + q) for p in range(STEPS) for q in range(grid_cols)
        ]
        wide.append(lax.ppermute(packed[r], axes, pairs))

    def exchange(col_own, row_own):
        cols = lax.all_gather(col_own, "row", axis=0, tiled=False)
        sides = []
        for d in range(grid_cols):
            pairs = []
            for g in range(group):
                for c in range(grid_cols):
                    for q in range(grid_cols):
                        source = (g * grid_cols + c) * grid_cols + q
                        target = (g * grid_cols + q) * grid_cols + (c + d) % grid_cols
                        pairs.append((source, target))
            sides.append(lax.ppermute(row_own, axes, pairs))
        return sides, cols

    nugget_rows = nugget.reshape(slots, 1, B)
    sides, cols, lowers = [], [], []

    def send(col_own, row_own):
        side, col = exchange(col_own, row_own)
        sides.append(side)
        cols.append(col)

    diag, panels, inverse, lower = open_group(tiles, tiles_of, GROUPS[0])
    lowers.append(lower)
    rest, col_own, row_own = solve_group(place, wide, panels, inverse, GROUPS[0])
    send(col_own, row_own)
    before = []
    for n in range(1, len(GROUPS)):
        made = factor_group(diag, rest, GROUPS[n], before, [*sides[n - 2], *cols[: 3 - n]] if n >= 2 else [])
        if n + 1 < len(GROUPS):
            diag, rest, *made = made
        col_own, row_own, lower = made
        lowers.append(lower)
        if n + 2 == len(GROUPS):
            before = [col_own, row_own]
        else:
            send(col_own, row_own)
    lower = jnp.concatenate(lowers)
    at = lax.dynamic_index_in_dim(lower, col_pos, 0, keepdims=False)
    matrix = trail(place, kernel, sides[:2], cols[:2], at, nugget_rows, False, grid_rows, grid_cols)
    at = lax.dynamic_index_in_dim(lower, jnp.minimum(col_pos + FIRST, STEPS - 1), 0, keepdims=False)
    return trail(place, matrix, sides[2:], cols[2:], at, nugget_rows, True, grid_rows, grid_cols)


def solution(mesh):
    return jax.shard_map(
        body,
        mesh=mesh,
        in_specs=(P("row", "col"), P("row")),
        out_specs=P("row", "col"),
        check_vma=False,
    )
```

```python
import functools

import jax
import jax.numpy as jnp
from jax import lax
from jax.experimental import pallas as pl
from jax.experimental.pallas import tpu as pltpu
from jax.sharding import PartitionSpec as P

B = 256
STEPS = 7
FIRST = 4
GROUPS = (1, 3, 2, 1)
STEP_COST = 100 * 10**9
SUB = 64
VMEM_LIMIT = 56 * 1024 * 1024


def assign_tiles(grid_cols):
    spare = STEPS
    sent, taken = {}, {}
    options = {}
    for a in range(STEPS):
        for b in range(a, STEPS):
            if b == a + grid_cols:
                sent[(a, b)] = (spare, a % grid_cols, 1, False)
                continue
            options[(a, b)] = [(a, b % grid_cols, b // grid_cols, False)]
            if a != b:
                options[(a, b)].append((b, a % grid_cols, a // grid_cols, True))

    def place(pair, seen):
        for option in options[pair]:
            device = option[:2]
            if device in seen:
                continue
            seen.add(device)
            if device not in taken or place(taken[device], seen):
                taken[device] = pair
                sent[pair] = option
                return True
        return False

    for pair in options:
        assert place(pair, set())
    return sent


def split(x):
    hi = x.astype(jnp.bfloat16)
    return hi, (x - hi.astype(jnp.float32)).astype(jnp.bfloat16)


def dot(a, b, dims=(1, 0)):
    return lax.dot_general(a, b, (((dims[0],), (dims[1],)), ((), ())), preferred_element_type=jnp.float32)


def dot_wide(a, b, dims=(1, 0)):
    a_hi, a_lo = split(a)
    b_hi, b_lo = split(b)
    return dot(a_hi, b_hi, dims) + (dot(a_hi, b_lo, dims) + dot(a_lo, b_hi, dims))


def eliminate(block):
    width = block.shape[1]
    count = SUB // 8
    rows = [block[8 * v : 8 * v + 8] for v in range(count)]
    sublane = lax.broadcasted_iota(jnp.int32, (8, width), 0)

    def lane(x, at):
        return jnp.broadcast_to(x[:, at : at + 1], (8, width))

    def row(x, at):
        return jnp.broadcast_to(x[at : at + 1], (8, width))

    for g in range(count):
        cols = [[lane(rows[v], 8 * g + m) for v in range(g, count)] for m in range(8)]
        pivot = {(a, b): row(cols[b][0], a) for b in range(8) for a in range(b, 8)}
        root, low = [None] * 8, {}
        for b in range(8):
            root[b] = lax.rsqrt(pivot[b, b])
            for a in range(b + 1, 8):
                low[a, b] = pivot[a, b] * root[b]
            for a in range(b + 1, 8):
                for c in range(b + 1, a + 1):
                    pivot[a, c] = pivot[a, c] - low[a, b] * low[c, b]
        inv = {}
        for b in range(8):
            inv[b, b] = root[b]
            for a in range(b + 1, 8):
                total = low[a, b] * inv[b, b]
                for m in range(b + 1, a):
                    total = total + low[a, m] * inv[m, b]
                inv[a, b] = -root[a] * total
        solved = None
        for b in range(8):
            coef = jnp.zeros((8, width), jnp.float32)
            for a in range(b, 8):
                coef = jnp.where(sublane == a, inv[a, b], coef)
            term = coef * row(rows[g], b)
            solved = term if solved is None else solved + term
        rows[g] = solved
        if g + 1 < count:
            across = [row(solved, m) for m in range(8)]
            for v in range(g + 1, count):
                total = None
                for m in range(8):
                    factor = inv[m, 0] * cols[0][v - g]
                    for b in range(1, m + 1):
                        factor = factor + inv[m, b] * cols[b][v - g]
                    term = factor * across[m]
                    total = term if total is None else total + term
                rows[v] = rows[v] - total
    return jnp.concatenate(rows, axis=0)


def factor_tile(work):
    eye = (
        lax.broadcasted_iota(jnp.int32, (SUB, 2 * SUB), 0) + SUB
        == lax.broadcasted_iota(jnp.int32, (SUB, 2 * SUB), 1)
    ).astype(jnp.float32)
    left = lax.broadcasted_iota(jnp.int32, (SUB, 2 * SUB), 1) < SUB
    for b in range(B // SUB):
        at = b * SUB
        base = at // (2 * SUB) * (2 * SUB)
        odd = at != base
        pair = work[at : at + SUB, base : base + 2 * SUB]
        if odd:
            pair = pltpu.roll(pair, SUB, 1)
        done = eliminate(jnp.where(left, pair, eye))
        moved = pltpu.roll(done, SUB, 1)
        inverse = moved[:, :SUB]
        end = B + base + 2 * SUB
        solved = dot_wide(inverse, work[at : at + SUB, base:end])
        if at + SUB < B:
            padded = jnp.where(left, 0.0, done) if odd else jnp.where(left, moved, 0.0)
            below = dot_wide(work[at + SUB : B, base : base + 2 * SUB], padded, (1, 1))
            start = (at + SUB) // (2 * SUB) * (2 * SUB)
            work[at + SUB : B, start:end] -= dot_wide(below, solved[:, start - base :])
        work[at : at + SUB, base:end] = solved


def read_tile(tile, turned):
    tile = tile[:B].astype(jnp.float32)
    return tile.T if turned else tile


def read_diagonal(packed):
    above = lax.broadcasted_iota(jnp.int32, (B, B), 0)
    beside = lax.broadcasted_iota(jnp.int32, (B, B), 1)
    packed = packed.astype(jnp.float32)
    tile = packed[:B]
    below = jnp.where(above > beside, tile + tile.T, 0.0)
    middle = jnp.where(above == beside, tile + packed[B : B + 1], 0.0)
    return below + below.T + middle


def factor_steps(held, panel, work, count, steps, stop, chunk, lower_ref, after):
    above = lax.broadcasted_iota(jnp.int32, (B, B), 0)
    beside = lax.broadcasted_iota(jnp.int32, (B, B), 1)

    def step(k, carry):
        at = pl.multiple_of(k * B, B)
        work[:, :B] = held[k, :, pl.ds(at, B)]
        work[:, B:] = (above == beside).astype(jnp.float32)
        factor_tile(work)
        lower_ref[k] = jnp.where(above >= beside, work[:, :B].T, 0.0)
        inv_hi, inv_lo = split(work[:, B:])

        def solve(c, carry):
            where = pl.ds(pl.multiple_of(c * chunk, chunk), chunk)
            hi, lo = split(held[k, :, where])
            panel[:, where] = (dot(inv_hi, hi) + (dot(inv_hi, lo) + dot(inv_lo, hi))).astype(jnp.bfloat16)
            return carry

        lax.fori_loop((k + 1) * (B // chunk), stop // chunk, solve, 0)
        after(k, at)

        def reduce(i, carry):
            side = panel[:, pl.ds(pl.multiple_of(i * B, B), B)].T
            held[i] -= dot(side, panel[...])
            return carry

        lax.fori_loop(k + 1, count, reduce, 0)
        return carry

    panel[...] = jnp.zeros_like(panel)
    lax.fori_loop(0, steps, step, 0)


def open_body(tiles_of, steps, tiles_ref, rest_ref, panel_ref, inverse_ref, lower_ref, held, panel, work):
    for (a, b), (index, turned) in tiles_of.items():
        tile = read_diagonal(tiles_ref[index]) if a == b else read_tile(tiles_ref[index], turned)
        held[a, :, b * B : (b + 1) * B] = tile

    def after(k, at):
        panel_ref[k] = panel[...]
        inverse_ref[k] = work[:, B:]

    factor_steps(held, panel, work, STEPS, steps, STEPS * B, B, lower_ref, after)
    rest_ref[...] = held[steps:, :, steps * B :]


def open_group(tiles, tiles_of, steps):
    f32, bf16 = jnp.float32, jnp.bfloat16
    whole = pl.BlockSpec(memory_space=pltpu.VMEM)
    left = STEPS - steps
    return pl.pallas_call(
        functools.partial(open_body, tiles_of, steps),
        out_shape=[
            jax.ShapeDtypeStruct((left, B, left * B), f32),
            jax.ShapeDtypeStruct((steps, B, STEPS * B), bf16),
            jax.ShapeDtypeStruct((steps, B, B), f32),
            jax.ShapeDtypeStruct((steps, B, B), f32),
        ],
        in_specs=[whole],
        out_specs=[whole] * 4,
        scratch_shapes=[
            pltpu.VMEM((STEPS, B, STEPS * B), f32),
            pltpu.VMEM((B, STEPS * B), bf16),
            pltpu.VMEM((B, 2 * B), f32),
        ],
        compiler_params=pltpu.CompilerParams(vmem_limit_bytes=VMEM_LIMIT),
        cost_estimate=pl.CostEstimate(flops=steps * STEP_COST, bytes_accessed=2**24, transcendentals=0),
        name="open_diagonal",
    )(tiles)


def solve_body(grid_rows, steps, place, *refs):
    wide_refs = refs[:grid_rows]
    panel_ref, inverse_ref, rest_ref, col_ref, row_ref, held = refs[grid_rows:]
    for r in range(grid_rows):
        held[place[0] ^ r] = wide_refs[r][...]
    for k in range(steps):
        own = dot_wide(inverse_ref[k], held[k]).astype(jnp.bfloat16)
        col_ref[k * B : (k + 1) * B, :] = own
        row_ref[:, k * B : (k + 1) * B] = own.T

        def reduce(i, carry):
            side = panel_ref[k, :, pl.ds(pl.multiple_of(i * B, B), B)].T
            held[i] -= dot(side, own)
            return carry

        lax.fori_loop(k + 1, STEPS, reduce, 0)
    rest_ref[...] = held[steps:STEPS]


def solve_group(place, wide, panels, inverse, steps):
    share = wide[0].shape[1]
    f32, bf16 = jnp.float32, jnp.bfloat16
    whole = pl.BlockSpec(memory_space=pltpu.VMEM)
    return pl.pallas_call(
        functools.partial(solve_body, len(wide), steps),
        out_shape=[
            jax.ShapeDtypeStruct((STEPS - steps, B, share), f32),
            jax.ShapeDtypeStruct((steps * B, share), bf16),
            jax.ShapeDtypeStruct((share, steps * B), bf16),
        ],
        in_specs=[pl.BlockSpec(memory_space=pltpu.SMEM)] + [whole] * (len(wide) + 2),
        out_specs=[whole] * 3,
        scratch_shapes=[pltpu.VMEM((len(wide), B, share), f32)],
        compiler_params=pltpu.CompilerParams(vmem_limit_bytes=VMEM_LIMIT),
        cost_estimate=pl.CostEstimate(flops=10**9, bytes_accessed=2**24, transcendentals=0),
        name="solve_rows",
    )(place, *wide, panels, inverse)


def factor_body(count, steps, share, chunk, earlier, waited, diag_ref, wide_ref, *refs):
    before, refs = refs[: 2 if earlier else 0], refs[(2 if earlier else 0) + waited :]
    if steps < count:
        rest_ref, rest_wide_ref, *refs = refs
    col_ref, row_ref, lower_ref, held, panel, work = refs
    edge = count * B
    held[:, :, :edge] = diag_ref[...]
    held[:, :, edge:] = wide_ref[...]
    if before:
        col_ref[:earlier, :] = before[0][...]
        row_ref[:, :earlier] = before[1][...]

    def after(k, at):
        own = panel[:, edge:]
        at = pl.multiple_of(at + earlier, B)
        col_ref[pl.ds(at, B), :] = own
        row_ref[:, pl.ds(at, B)] = own.T

    factor_steps(held, panel, work, count, steps, edge + share, chunk, lower_ref, after)
    if steps < count:
        rest_ref[...] = held[steps:, :, steps * B : edge]
        rest_wide_ref[...] = held[steps:, :, edge:]


def factor_group(diag, wide, steps, before, waited):
    count, _, share = wide.shape
    f32, bf16 = jnp.float32, jnp.bfloat16
    earlier = before[0].shape[0] if before else 0
    outs = [
        jax.ShapeDtypeStruct((earlier + steps * B, share), bf16),
        jax.ShapeDtypeStruct((share, earlier + steps * B), bf16),
        jax.ShapeDtypeStruct((steps, B, B), f32),
    ]
    left = count - steps
    if left:
        outs = [
            jax.ShapeDtypeStruct((left, B, left * B), f32),
            jax.ShapeDtypeStruct((left, B, share), f32),
        ] + outs
    whole = pl.BlockSpec(memory_space=pltpu.VMEM)
    return pl.pallas_call(
        functools.partial(factor_body, count, steps, share, min(B, share), earlier, len(waited)),
        out_shape=outs,
        in_specs=[whole] * (2 + len(before)) + [pl.BlockSpec(memory_space=pl.ANY)] * len(waited),
        out_specs=[whole] * len(outs),
        scratch_shapes=[
            pltpu.VMEM((count, B, count * B + share), f32),
            pltpu.VMEM((B, count * B + share), bf16),
            pltpu.VMEM((B, 2 * B), f32),
        ],
        compiler_params=pltpu.CompilerParams(vmem_limit_bytes=VMEM_LIMIT),
        cost_estimate=pl.CostEstimate(flops=steps * STEP_COST, bytes_accessed=2**24, transcendentals=0),
        name="factor",
    )(diag, wide, *before, *waited)


def pack_body(place, kernel_ref, out_ref):
    out_ref[0] = kernel_ref[...]


def pack(place, kernel, grid_rows, grid_cols, share):
    group = grid_rows // grid_cols
    width = min(B, share)

    def source(r, j, place):
        chunk = place[0] ^ r
        at = chunk % grid_cols * share + j * width
        return (0, ((at // B * group + chunk // grid_cols) * B + at % B) // width)

    return pl.pallas_call(
        pack_body,
        out_shape=jax.ShapeDtypeStruct((grid_rows, B, share), jnp.float32),
        grid_spec=pltpu.PrefetchScalarGridSpec(
            num_scalar_prefetch=1,
            grid=(grid_rows, share // width),
            in_specs=[pl.BlockSpec((B, width), source)],
            out_specs=pl.BlockSpec((1, B, width), lambda r, j, place: (r, 0, j)),
        ),
        cost_estimate=pl.CostEstimate(flops=0, bytes_accessed=2**23, transcendentals=0),
        name="pack",
    )(place, kernel)


def trail_body(last, parts, grid_rows, grid_cols, slots, width, *refs):
    place, prev_ref, *sides = refs[: 2 + parts * grid_cols]
    col_refs = refs[2 + parts * grid_cols : 2 + parts * (grid_cols + 1)]
    lower_ref, nugget_ref = refs[2 + parts * (grid_cols + 1) :][:2]
    out_ref = refs[-1]
    sides = [sides[n * grid_cols : (n + 1) * grid_cols] for n in range(parts)]
    row_pos, col_pos = place[0], place[1]
    share = sides[0][0].shape[0]
    skip = B // width if last else 0
    start = (pl.program_id(0) + skip) * width
    slot, inner = start // B, pl.multiple_of(start % B, width)

    def rows_of(d):
        return pl.ds(pl.multiple_of(lax.rem(col_pos - d + grid_cols, grid_cols) * share, share), share)

    def product():
        for d in range(grid_cols):
            total = dot(sides[0][d][...], col_refs[0][0])
            for n in range(1, parts):
                total = total + dot(sides[n][d][...], col_refs[n][0])
            out_ref[rows_of(d), :] = prev_ref[rows_of(d), :] - total

    def panel():
        first = 0
        for n in range(parts):
            wide = sides[n][0].shape[1] // B

            @pl.when((col_pos >= first) & (col_pos < first + wide))
            def _():
                at = pl.multiple_of((col_pos - first) * B + inner, width)
                for d in range(grid_cols):
                    out_ref[rows_of(d), :] = sides[n][d][:, pl.ds(at, width)].astype(jnp.float32)

            first += wide
        step = col_pos + (FIRST if last else 0)

        @pl.when(row_pos == step)
        def _():
            out_ref[:B, :] = lower_ref[:, pl.ds(inner, width)]

        @pl.when(row_pos < step)
        def _():
            out_ref[:B, :] = jnp.zeros((B, width), jnp.float32)

    if last:
        in_panel = (slot == 1) & (col_pos + FIRST < STEPS)
        pl.when(in_panel)(panel)

        @pl.when(jnp.logical_not(in_panel))
        def _():
            product()

            @pl.when(row_pos < STEPS)
            def _():
                out_ref[:B, :] = jnp.zeros((B, width), jnp.float32)

    else:
        pl.when(slot == 0)(panel)

        @pl.when(slot > 0)
        def _():
            product()
            offset = slot * grid_cols + col_pos - row_pos
            level = offset // grid_rows

            @pl.when((offset >= 0) & (lax.rem(offset, grid_rows) == 0) & (level < slots))
            def _():
                own = pl.ds(pl.multiple_of(level * B, B), B)
                same = lax.broadcasted_iota(jnp.int32, (B, width), 0) == (
                    lax.broadcasted_iota(jnp.int32, (B, width), 1) + inner
                )
                value = nugget_ref[level, :, pl.ds(inner, width)]
                out_ref[own, :] += jnp.where(same, value, 0.0)


def trail(place, prev, sides, cols, lower, nugget, last, grid_rows, grid_cols):
    rows_here, cols_here = prev.shape
    share = sides[0][0].shape[0]
    depths = [part[0].shape[1] for part in sides]
    width = min(B, share)
    slots = rows_here // B
    group = grid_rows // grid_cols
    skip = B // width if last else 0

    def col_block(u, place):
        start = (u + skip) * width
        slot, inner = start // B, start % B
        at = slot // group * B + inner
        return (slot % group * grid_cols + at // share, 0, at % share // width)

    def own_block(u, place):
        return (0, u + skip)

    block = pl.BlockSpec((rows_here, width), own_block)
    return pl.pallas_call(
        functools.partial(trail_body, last, len(sides), grid_rows, grid_cols, slots, width),
        out_shape=jax.ShapeDtypeStruct(prev.shape, jnp.float32),
        grid_spec=pltpu.PrefetchScalarGridSpec(
            num_scalar_prefetch=1,
            grid=(cols_here // width - skip,),
            in_specs=[block]
            + [pl.BlockSpec((share, depth), lambda u, place: (0, 0)) for depth in depths for _ in range(grid_cols)]
            + [pl.BlockSpec((1, depth, width), col_block) for depth in depths]
            + [
                pl.BlockSpec((B, B), lambda u, place: (0, 0)),
                pl.BlockSpec((slots, 1, B), lambda u, place: (0, 0, 0)),
            ],
            out_specs=block,
        ),
        input_output_aliases={1: 0} if last else {},
        compiler_params=pltpu.CompilerParams(
            vmem_limit_bytes=VMEM_LIMIT, dimension_semantics=("arbitrary",)
        ),
        cost_estimate=pl.CostEstimate(
            flops=2 * rows_here * cols_here * sum(depths),
            bytes_accessed=8 * rows_here * cols_here,
            transcendentals=0,
        ),
        name="trail",
    )(place, prev, *[x for part in sides for x in part], *cols, lower, nugget)


def body(kernel, nugget):
    rows_here, cols_here = kernel.shape
    grid_rows = lax.axis_size("row")
    grid_cols = lax.axis_size("col")
    row_pos = lax.axis_index("row")
    col_pos = lax.axis_index("col")
    group = grid_rows // grid_cols
    share = rows_here // grid_cols
    slots = rows_here // B
    axes = ("row", "col")
    place = jnp.stack([row_pos, col_pos]).astype(jnp.int32)

    sent = assign_tiles(grid_cols)
    picked = [[0] * grid_cols for _ in range(grid_rows)]
    for row, col, slot, _ in sent.values():
        picked[row][col] = slot if row < STEPS else 0
    near, far = kernel[:B, :B], kernel[:B, B : 2 * B]
    passed = lax.ppermute(
        far.astype(jnp.bfloat16),
        axes,
        [(a * grid_cols + a % grid_cols, STEPS * grid_cols + a % grid_cols) for a in range(STEPS - grid_cols)],
    )
    pick = jnp.asarray(picked, jnp.int32)[row_pos, col_pos]
    mine = jnp.where(pick == 1, far, near)
    on_diagonal = (row_pos < STEPS) & (row_pos == pick * grid_cols + col_pos)
    across, down = jnp.arange(B)[None, :], jnp.arange(B)[:, None]
    tile = mine + jnp.where(down == across, nugget[:B][:, None], jnp.float32(0.0))
    kept = lax.reduce_precision(tile, exponent_bits=8, mantissa_bits=7)
    remainder = tile - kept
    tile = jnp.where(down >= across, kept, remainder.T)
    middle = jnp.sum(jnp.where(down == across, remainder, 0.0), axis=0, keepdims=True)
    mine = jnp.where(on_diagonal, tile, mine).astype(jnp.bfloat16)
    mine = jnp.where(row_pos == STEPS, passed, mine)
    mine = jnp.concatenate([mine, jnp.broadcast_to(middle, (16, B)).astype(jnp.bfloat16)])
    tiles = lax.all_gather(mine, axes, axis=0, tiled=False)[: (STEPS + 1) * grid_cols]
    tiles_of = {pair: (row * grid_cols + col, turned) for pair, (row, col, _, turned) in sent.items()}

    packed = pack(place, kernel, grid_rows, grid_cols, share)
    wide = [packed[0]]
    for r in range(1, grid_rows):
        pairs = [
            (p * grid_cols + q, (p ^ r) * grid_cols + q) for p in range(STEPS) for q in range(grid_cols)
        ]
        wide.append(lax.ppermute(packed[r], axes, pairs))

    def exchange(col_own, row_own):
        cols = lax.all_gather(col_own, "row", axis=0, tiled=False)
        sides = []
        for d in range(grid_cols):
            pairs = []
            for g in range(group):
                for c in range(grid_cols):
                    for q in range(grid_cols):
                        source = (g * grid_cols + c) * grid_cols + q
                        target = (g * grid_cols + q) * grid_cols + (c + d) % grid_cols
                        pairs.append((source, target))
            sides.append(lax.ppermute(row_own, axes, pairs))
        return sides, cols

    nugget_rows = nugget.reshape(slots, 1, B)
    sides, cols, lowers = [], [], []

    def send(col_own, row_own):
        side, col = exchange(col_own, row_own)
        sides.append(side)
        cols.append(col)

    diag, panels, inverse, lower = open_group(tiles, tiles_of, GROUPS[0])
    lowers.append(lower)
    rest, col_own, row_own = solve_group(place, wide, panels, inverse, GROUPS[0])
    send(col_own, row_own)
    before = []
    for n in range(1, len(GROUPS)):
        made = factor_group(diag, rest, GROUPS[n], before, [*sides[n - 2], *cols[: 3 - n]] if n >= 2 else [])
        if n + 1 < len(GROUPS):
            diag, rest, *made = made
        col_own, row_own, lower = made
        lowers.append(lower)
        if n + 2 == len(GROUPS):
            before = [col_own, row_own]
        else:
            send(col_own, row_own)
    lower = jnp.concatenate(lowers)
    at = lax.dynamic_index_in_dim(lower, col_pos, 0, keepdims=False)
    matrix = trail(place, kernel, sides[:2], cols[:2], at, nugget_rows, False, grid_rows, grid_cols)
    at = lax.dynamic_index_in_dim(lower, jnp.minimum(col_pos + FIRST, STEPS - 1), 0, keepdims=False)
    return trail(place, matrix, sides[2:], cols[2:], at, nugget_rows, True, grid_rows, grid_cols)


def solution(mesh):
    return jax.shard_map(
        body,
        mesh=mesh,
        in_specs=(P("row", "col"), P("row")),
        out_specs=P("row", "col"),
        check_vma=False,
    )
```
